32 devices in a mesh: pair: 16 (over z, y, x), sector: 2 (over core).
Axes of the slice: x: 2, y: 2, z: 4, core: 2. Of those that a mesh axis runs over, the one named last changes fastest.
Arguments:
- site_tensor: bfloat16 [4, 16, 128, 128], P(None, 'sector', 'pair'), may hold values from -0.5 to 0.5
- operators: bfloat16 [384, 16, 128, 128], P('pair', 'sector'), may hold values from -6 to 6
- one_index: bfloat16 [32, 16, 128, 128], P('pair', 'sector'), may hold values from -6 to 6
- weights: bfloat16 [384, 32], P('pair'), may hold values from -2 to 2
- comp_charge: int32 [384], P('pair'), may hold values from 0 to 2
- one_charge: int32 [32], replicated, may hold values from 0 to 2
- sector_size: int32 [16], replicated, may hold values from 1 to 128, 1280 in all
- coupling: int32 [16, 4], replicated, may hold values from 0 to 16, as said below
Outputs:
- renormalized: bfloat16 [384, 16, 128, 128], P('pair', 'sector')
The draws below stay inside these ranges and needn't reach their ends.
Inputs may be any that keep to these rules, and one draw needn't show every extreme that they name: coupling[s, t] = min(s + c[t], 16) where c is an arrangement of the charges 0, 1, 1, 2 over the 4 orbital states; the value 16 marks a dropped combination.
All inputs are finite; a program needn't handle non-finite values.
Results may differ from the reference program's by a relative error of at most 0.007.
Values may be sent and summed in bfloat16 or wider, within the bound.
A program may use at most 128 MiB of HBM per device.

```python
import math
import jax
import jax.numpy as jnp
import numpy as np
from jax import lax

S = 16
B = 128
DLOC = 4
OPERATORS = 384
ONE_OPS = 32


def draw_coupling(key, part):
    order = jax.random.permutation(jax.random.fold_in(key, 7), DLOC)
    charge_table = jnp.array([0, 1, 1, 2], jnp.int32)
    charges = jnp.take(charge_table, order)
    sectors = jnp.arange(S, dtype=jnp.int32)[:, None]
    return jnp.minimum(sectors + charges[None, :], S).astype(jnp.int32)


def plant(values, rng, low, largest):
    extent = values.shape
    place = [jax.random.randint(jax.random.fold_in(rng, axis), (), 0, extent[axis]) for axis in range(len(extent))]
    values = values.at[tuple(place)].set(low)
    longest = extent.index(max(extent))
    place[longest] = (place[longest] + 1) % extent[longest]
    return values.at[tuple(place)].set(largest)


def shard_levels(key, extent, shards, low, largest):
    level, own = 1.0, jax.random.fold_in(key, 6)
    for dim, parts in shards:
        steps = jnp.exp(jax.random.uniform(jax.random.fold_in(own, dim), (parts,), jnp.float32, low / len(shards), largest / len(shards)))
        level = level * jnp.repeat(steps, extent[dim] // parts).reshape([-1 if axis == dim else 1 for axis in range(len(extent))])
    return level


def length_profile(count, total, bound, lean):
    loads = [(1 << 20) // math.isqrt(grade ** lean) + 1 for grade in range(2, count + 1)]
    surplus, holding = total - bound - (count - 1), [1] * (count - 1)
    while surplus > 0:
        movable = [i for i in range(count - 1) if holding[i] < bound]
        pool, remaining = sum([loads[i] for i in movable]), surplus
        for i in movable:
            addition = min(bound - holding[i], max(1, remaining * loads[i] // pool), surplus)
            holding[i] = holding[i] + addition
            surplus = surplus - addition
    return np.array([bound] + holding)


def ragged(own_key, number_of, total, reach, skew):
    if number_of == 2:
        one = jax.random.randint(own_key, (), max(1, total - reach), min(reach, total - 1) + 1)
        return jnp.stack([one, total - one])
    sizes = jnp.asarray(length_profile(number_of, total, reach, skew), jnp.int32)
    pairs = (number_of - 1) // 2
    source_of, sink = sizes[1:1 + 2 * pairs:2], sizes[2:2 + 2 * pairs:2]
    slack = jnp.minimum(source_of - 1, reach - sink)
    passed = jax.random.randint(jax.random.fold_in(own_key, 1), (pairs,), 0, 1 << 20) % (slack + 1)
    sizes = sizes.at[1:1 + 2 * pairs:2].set(source_of - passed).at[2:2 + 2 * pairs:2].set(sink + passed)
    return sizes[jax.random.permutation(jax.random.fold_in(own_key, 2), number_of)]


def bell_draw(own_key, shape, scale, most, pieces=(), kind=jnp.bfloat16):
    values = scale * jax.random.normal(own_key, shape, jnp.float32)
    if pieces:
        values = values * shard_levels(own_key, shape, pieces, -0.22, 0.18)
    return jnp.clip(values, -most, most).astype(kind)


def setup_inputs(seed: int = 0) -> dict:
    key_list = jax.random.split(jax.random.key(seed), 9)
    return {
        "site_tensor": bell_draw(key_list[0], (DLOC, S, B, B), B ** -0.5, 0.5, ((1, 2), (2, 16))),
        "operators": bell_draw(key_list[1], (OPERATORS, S, B, B), 1.0, 6.0, ((0, 16), (1, 2))),
        "one_index": bell_draw(key_list[2], (ONE_OPS, S, B, B), 1.0, 6.0, ((0, 16), (1, 2))),
        "weights": bell_draw(key_list[3], (OPERATORS, ONE_OPS), (ONE_OPS // 3) ** -0.5, 2.0, ((0, 16),)),
        "comp_charge": plant(jax.random.randint(key_list[4], (OPERATORS,), 0, 3), jax.random.fold_in(key_list[4], 1), 0, 2).astype(jnp.int32),
        "one_charge": plant(jax.random.randint(key_list[5], (ONE_OPS,), 0, 3), jax.random.fold_in(key_list[5], 1), 0, 2).astype(jnp.int32),
        "sector_size": ragged(key_list[6], S, S * B * 5 // 8, B, 1).astype(jnp.int32),
        "coupling": draw_coupling(jax.random.fold_in(key_list[8], 71), 0),
    }


def reference(site_tensor, operators, one_index, weights, comp_charge, one_charge, sector_size, coupling):
    positions = jnp.arange(B, dtype=jnp.int32)
    live_rows = positions[None, :] < sector_size[:, None]
    masked = jnp.where(live_rows[None, :, :, None], site_tensor, jnp.zeros((), jnp.bfloat16))
    matching = comp_charge[:, None] == one_charge[None, :]
    coef = jnp.where(matching, weights, jnp.zeros((), jnp.bfloat16))

    def build(sector):
        own_ops = operators[:, sector]
        own_one = one_index[:, sector]
        summed = jnp.dot(coef, own_one.reshape(ONE_OPS, B * B), preferred_element_type=jnp.float32)
        return (own_ops.astype(jnp.float32) + summed.reshape(OPERATORS, B, B)).astype(jnp.bfloat16)

    combined = lax.map(build, jnp.arange(S, dtype=jnp.int32))
    state_charge = coupling[0]

    def new_sector(target):
        total = jnp.zeros((OPERATORS, B, B), jnp.float32)
        for local_state in range(DLOC):
            source = target - state_charge[local_state]
            usable = source >= 0
            clipped = jnp.clip(source, 0, S - 1).astype(jnp.int32)
            left_block = masked[local_state, clipped]
            right_index = clipped + comp_charge
            in_range = right_index < S
            right_blocks = masked[local_state, jnp.clip(right_index, 0, S - 1).astype(jnp.int32)]
            right_blocks = jnp.where(in_range[:, None, None], right_blocks, jnp.zeros((), jnp.bfloat16))
            partial_value = jnp.einsum("kij,kjc->kic", combined[clipped].astype(jnp.float32), right_blocks.astype(jnp.float32), precision=lax.Precision.HIGHEST).astype(jnp.bfloat16)
            contrib = jnp.einsum("ia,kic->kac", left_block.astype(jnp.float32), partial_value.astype(jnp.float32), precision=lax.Precision.HIGHEST)
            total = total + jnp.where(usable, contrib, jnp.zeros((), jnp.float32))
        return total.astype(jnp.bfloat16)

    result = lax.map(new_sector, jnp.arange(S, dtype=jnp.int32))
    return jnp.transpose(result, (1, 0, 2, 3))
```

```python
import jax
import jax.numpy as jnp
from jax import lax
from jax.experimental import pallas as pl
from jax.experimental.pallas import tpu as pltpu
from jax.sharding import PartitionSpec as P

ROWS = 16
REACH = 2


def from_behind(value, axis, steps):
    count = lax.axis_size(axis)
    initial, last = (max(0, -steps), min(count, count - steps))
    return lax.ppermute(value, axis, [(source, source + steps) for source in range(initial, last)])


def renormalize(sec_local, charge, shift, ops, ones, kron, pool, left, out, carry, comb, inner):
    step = pl.program_id(0)
    count, _, size, _ = ops.shape
    one_count = ones.shape[0]
    states = left.shape[0]

    @pl.when(step < sec_local)
    def _():
        for base in range(0, size, 2 * ROWS):
            rows = jnp.concatenate(
                [
                    ones[:, 0, start : start + ROWS, :].reshape(one_count * ROWS, size)
                    for start in (base, base + ROWS)
                ],
                axis=1,
            )
            added = jnp.dot(kron[...], rows, preferred_element_type=jnp.float32)
            for half in range(2):
                start = base + half * ROWS
                part = added[:, half * size : (half + 1) * size].reshape(count, ROWS, size)
                comb[:, start : start + ROWS, :] = (
                    ops[:, 0, start : start + ROWS, :].astype(jnp.float32) + part
                ).astype(jnp.bfloat16)
        slot = lax.rem(step, REACH + 1)

        def one(k, _):
            right = pool[step + charge[k]]
            value = jnp.dot(comb[k], right, preferred_element_type=jnp.float32)
            inner[slot, k] = value.astype(jnp.bfloat16)
            return 0

        lax.fori_loop(0, count, one, 0, unroll=4)

    lefts, slots = [], []
    for t in range(states):
        source = step - shift[t]
        legal = jnp.logical_and(source >= 0, source < sec_local)
        source = jnp.clip(source, 0, sec_local - 1)
        block = left[t, source]
        lefts.append(jnp.where(legal, block, jnp.zeros_like(block)))
        slots.append(lax.rem(source, REACH + 1))
    lhs = jnp.concatenate(lefts, axis=1)

    def emit(target):
        def two(pair, _):
            rhs = jnp.concatenate(
                [
                    jnp.concatenate(
                        [
                            inner[slots[t], 2 * pair + h, :, t * size : (t + 1) * size]
                            for t in range(states)
                        ],
                        axis=0,
                    )
                    for h in range(2)
                ],
                axis=1,
            )
            value = jnp.dot(lhs, rhs, preferred_element_type=jnp.float32)
            for h in range(2):
                target[2 * pair + h, 0] = value[:, h * size : (h + 1) * size].astype(jnp.bfloat16)
            return 0

        lax.fori_loop(0, count // 2, two, 0, unroll=2)

    @pl.when(step < sec_local)
    def _():
        emit(out)

    @pl.when(step >= sec_local)
    def _():
        emit(carry)


def body(
    site_tensor, operators, one_index, weights, comp_charge, one_charge, sector_size, coupling
):
    count, sec_local, size, _ = operators.shape
    states = site_tensor.shape[0]
    first_sector = lax.axis_index("sector") * sec_local
    gathered_site = lax.all_gather(site_tensor, "pair", axis=0)
    all_ones = lax.all_gather(one_index, "pair", axis=0, tiled=True)
    full_site = jnp.transpose(gathered_site, (1, 2, 0, 3, 4)).reshape(states, sec_local, size, size)
    own_sizes = lax.dynamic_slice_in_dim(sector_size, first_sector, sec_local)
    live_rows = jnp.arange(size, dtype=jnp.int32)[None, :] < own_sizes[:, None]
    own_site = jnp.where(live_rows[None, :, :, None], full_site, jnp.zeros((), jnp.bfloat16))
    upper = from_behind(own_site[:, :REACH], "sector", -1)
    pool = jnp.concatenate([own_site, upper], axis=1)
    pool = jnp.transpose(pool, (1, 2, 0, 3)).reshape(sec_local + REACH, size, states * size)
    left = jnp.swapaxes(own_site, 2, 3)
    matching = comp_charge[:, None] == one_charge[None, :]
    coef = jnp.where(matching, weights, jnp.zeros((), jnp.bfloat16))
    one_count = coef.shape[1]
    unit = jnp.eye(ROWS, dtype=jnp.bfloat16)
    kron = (coef[:, None, :, None] * unit[None, :, None, :]).reshape(
        count * ROWS, one_count * ROWS
    )

    def held(shape):
        return pl.BlockSpec(shape, lambda i, *_: (0,) * len(shape))

    def last(i):
        return jnp.minimum(i, sec_local - 1)

    out, carry = pl.pallas_call(
        lambda *refs: renormalize(sec_local, *refs),
        grid_spec=pltpu.PrefetchScalarGridSpec(
            num_scalar_prefetch=2,
            grid=(sec_local + REACH,),
            in_specs=[
                pl.BlockSpec((count, 1, size, size), lambda i, *_: (0, last(i), 0, 0)),
                pl.BlockSpec((one_count, 1, size, size), lambda i, *_: (0, last(i), 0, 0)),
                held(kron.shape),
                held(pool.shape),
                held(left.shape),
            ],
            out_specs=[
                pl.BlockSpec((count, 1, size, size), lambda i, *_: (0, last(i), 0, 0)),
                pl.BlockSpec(
                    (count, 1, size, size),
                    lambda i, *_: (0, jnp.maximum(i - sec_local, 0), 0, 0),
                ),
            ],
            scratch_shapes=[
                pltpu.VMEM((count, size, size), jnp.bfloat16),
                pltpu.VMEM((REACH + 1, count, size, states * size), jnp.bfloat16),
            ],
        ),
        out_shape=[
            jax.ShapeDtypeStruct(operators.shape, jnp.bfloat16),
            jax.ShapeDtypeStruct((count, REACH, size, size), jnp.bfloat16),
        ],
        compiler_params=pltpu.CompilerParams(vmem_limit_bytes=48 * 2**20),
    )(comp_charge, coupling[0], operators, all_ones, kron, pool, left)
    carried = from_behind(carry, "sector", 1)
    return out.at[:, :REACH].add(carried)


def solution(mesh):
    return jax.shard_map(
        body,
        mesh=mesh,
        in_specs=(
            P(None, "sector", "pair", None),
            P("pair", "sector", None, None),
            P("pair", "sector", None, None),
            P("pair", None),
            P("pair"),
            P(),
            P(),
            P(),
        ),
        out_specs=P("pair", "sector", None, None),
        check_vma=False,
    )
```

```python
import jax
import jax.numpy as jnp
from jax import lax
from jax.experimental import pallas as pl
from jax.experimental.pallas import tpu as pltpu
from jax.sharding import PartitionSpec as P

ROWS = 16
REACH = 2


def from_behind(value, axis, steps):
    count = lax.axis_size(axis)
    initial, last = (max(0, -steps), min(count, count - steps))
    return lax.ppermute(value, axis, [(source, source + steps) for source in range(initial, last)])


def renormalize(sec_local, charge, shift, ops, ones, kron, pool, left, out, carry, comb, inner):
    step = pl.program_id(0)
    count, _, size, _ = ops.shape
    one_count = ones.shape[0]
    states = left.shape[0]

    @pl.when(step < sec_local)
    def _():
        for base in range(0, size, 2 * ROWS):
            rows = jnp.concatenate(
                [
                    ones[:, 0, start : start + ROWS, :].reshape(one_count * ROWS, size)
                    for start in (base, base + ROWS)
                ],
                axis=1,
            )
            added = jnp.dot(kron[...], rows, preferred_element_type=jnp.float32)
            for half in range(2):
                start = base + half * ROWS
                part = added[:, half * size : (half + 1) * size].reshape(count, ROWS, size)
                comb[:, start : start + ROWS, :] = (
                    ops[:, 0, start : start + ROWS, :].astype(jnp.float32) + part
                ).astype(jnp.bfloat16)
        slot = lax.rem(step, REACH + 1)

        def one(k, _):
            right = pool[step + charge[k]]
            value = jnp.dot(comb[k], right, preferred_element_type=jnp.float32)
            inner[slot, k] = value.astype(jnp.bfloat16)
            return 0

        lax.fori_loop(0, count, one, 0, unroll=4)

    lefts, slots = [], []
    for t in range(states):
        source = step - shift[t]
        legal = jnp.logical_and(source >= 0, source < sec_local)
        source = jnp.clip(source, 0, sec_local - 1)
        block = left[t, source]
        lefts.append(jnp.where(legal, block, jnp.zeros_like(block)))
        slots.append(lax.rem(source, REACH + 1))
    lhs = jnp.concatenate(lefts, axis=1)

    def emit(target):
        def two(pair, _):
            rhs = jnp.concatenate(
                [
                    jnp.concatenate(
                        [
                            inner[slots[t], 2 * pair + h, :, t * size : (t + 1) * size]
                            for t in range(states)
                        ],
                        axis=0,
                    )
                    for h in range(2)
                ],
                axis=1,
            )
            value = jnp.dot(lhs, rhs, preferred_element_type=jnp.float32)
            for h in range(2):
                target[2 * pair + h, 0] = value[:, h * size : (h + 1) * size].astype(jnp.bfloat16)
            return 0

        lax.fori_loop(0, count // 2, two, 0, unroll=2)

    @pl.when(step < sec_local)
    def _():
        emit(out)

    @pl.when(step >= sec_local)
    def _():
        emit(carry)


def factors(count):
    short = 1 << ((count.bit_length() - 1) // 3)
    return (count // (short * short), short, short)


def gather_both(dims, classes, site, ones, all_site, all_ones, send_sem, recv_sem, own_sem):
    me = lax.axis_index("pair")
    strides = (dims[1] * dims[2], dims[2], 1)
    mine = [lax.rem(lax.div(me, strides[d]), dims[d]) for d in range(3)]

    def moved(place, d, r):
        other = lax.rem(mine[d] + r, dims[d])
        return place + (other - mine[d]) * strides[d]

    barrier = pltpu.get_barrier_semaphore()
    greeted = 0
    for d in range(3):
        for r in range(1, dims[d]):
            pl.semaphore_signal(
                barrier,
                inc=1,
                device_id={"pair": moved(me, d, r)},
                device_id_type=pl.DeviceIdType.MESH,
            )
            greeted += 1
    keep = [
        pltpu.make_async_copy(site, all_site.at[me], own_sem.at[0]),
        pltpu.make_async_copy(ones, all_ones.at[me], own_sem.at[1]),
    ]
    for copy in keep:
        copy.start()
    pl.semaphore_wait(barrier, greeted)

    sent = []

    def piece(c, block, own):
        slabs = classes[c][1]
        if slabs is None:
            return site if own else all_site.at[block]
        part = pl.ds(*slabs)
        return ones.at[part] if own else all_ones.at[block, part]

    def send(c, block, own, stages):
        for d in stages:
            for r in range(1, dims[d]):
                copy = pltpu.make_async_remote_copy(
                    src_ref=piece(c, block, own),
                    dst_ref=piece(c, block, False),
                    send_sem=send_sem.at[len(sent)],
                    recv_sem=recv_sem.at[c, block],
                    device_id={"pair": moved(me, d, r)},
                    device_id_type=pl.DeviceIdType.MESH,
                )
                copy.start()
                sent.append(copy)

    def arrive(c, block):
        pltpu.make_async_remote_copy(
            src_ref=piece(c, block, False),
            dst_ref=piece(c, block, False),
            send_sem=send_sem.at[0],
            recv_sem=recv_sem.at[c, block],
            device_id={"pair": moved(me, 2, 1)},
            device_id_type=pl.DeviceIdType.MESH,
        ).wait_recv()

    for c, (order, _) in enumerate(classes):
        send(c, me, True, order)
    for stage in range(3):
        rounds = []
        for c, (order, _) in enumerate(classes):
            steps = []
            places = [me]
            for d in order[:stage]:
                places = [moved(p, d, r) for r in range(dims[d]) for p in places]
            for r in range(1, dims[order[stage]]):
                steps += [(c, moved(p, order[stage], r)) for p in places]
            rounds.append(steps)
        for i in range(max(len(steps) for steps in rounds)):
            for steps in rounds:
                if i < len(steps):
                    c, block = steps[i]
                    arrive(c, block)
                    send(c, block, False, classes[c][0][stage + 1 :])
    for copy in sent:
        copy.wait_send()
    for copy in keep:
        copy.wait()


def gather(site_tensor, one_index):
    count = lax.axis_size("pair")
    dims = factors(count)
    size = site_tensor.shape[-1]
    site = site_tensor.reshape(-1, size)
    ones = one_index.reshape(-1, size, size)
    slabs = ones.shape[0]
    late = slabs // REACH // 8
    early = (slabs - 2 * late) // 2
    classes = [((0, 1, 2), None)]
    first = 0
    for order, number in (
        ((0, 1, 2), early),
        ((0, 2, 1), slabs - 2 * late - early),
        ((2, 1, 0), late),
        ((1, 2, 0), late),
    ):
        if number:
            classes.append((order, (first, number)))
        first += number
    all_site, all_ones = pl.pallas_call(
        lambda *refs: gather_both(dims, classes, *refs),
        in_specs=[pl.BlockSpec(memory_space=pl.ANY)] * 2,
        out_specs=[pl.BlockSpec(memory_space=pl.ANY)] * 2,
        out_shape=[
            jax.ShapeDtypeStruct((count,) + site.shape, site.dtype),
            jax.ShapeDtypeStruct((count,) + ones.shape, ones.dtype),
        ],
        scratch_shapes=[
            pltpu.SemaphoreType.DMA((len(classes) * (count - 1),)),
            pltpu.SemaphoreType.DMA((len(classes), count)),
            pltpu.SemaphoreType.DMA((2,)),
        ],
        compiler_params=pltpu.CompilerParams(
            collective_id=0, has_side_effects=True, vmem_limit_bytes=48 * 2**20
        ),
    )(site, ones)
    return (
        all_site.reshape((count,) + site_tensor.shape),
        all_ones.reshape((-1,) + one_index.shape[1:]),
    )


def body(
    site_tensor, operators, one_index, weights, comp_charge, one_charge, sector_size, coupling
):
    count, sec_local, size, _ = operators.shape
    states = site_tensor.shape[0]
    first_sector = lax.axis_index("sector") * sec_local
    gathered_site, all_ones = gather(site_tensor, one_index)
    full_site = jnp.transpose(gathered_site, (1, 2, 0, 3, 4)).reshape(states, sec_local, size, size)
    own_sizes = lax.dynamic_slice_in_dim(sector_size, first_sector, sec_local)
    live_rows = jnp.arange(size, dtype=jnp.int32)[None, :] < own_sizes[:, None]
    own_site = jnp.where(live_rows[None, :, :, None], full_site, jnp.zeros((), jnp.bfloat16))
    upper = from_behind(own_site[:, :REACH], "sector", -1)
    pool = jnp.concatenate([own_site, upper], axis=1)
    pool = jnp.transpose(pool, (1, 2, 0, 3)).reshape(sec_local + REACH, size, states * size)
    left = jnp.swapaxes(own_site, 2, 3)
    matching = comp_charge[:, None] == one_charge[None, :]
    coef = jnp.where(matching, weights, jnp.zeros((), jnp.bfloat16))
    one_count = coef.shape[1]
    unit = jnp.eye(ROWS, dtype=jnp.bfloat16)
    kron = (coef[:, None, :, None] * unit[None, :, None, :]).reshape(
        count * ROWS, one_count * ROWS
    )

    def held(shape):
        return pl.BlockSpec(shape, lambda i, *_: (0,) * len(shape))

    def last(i):
        return jnp.minimum(i, sec_local - 1)

    out, carry = pl.pallas_call(
        lambda *refs: renormalize(sec_local, *refs),
        grid_spec=pltpu.PrefetchScalarGridSpec(
            num_scalar_prefetch=2,
            grid=(sec_local + REACH,),
            in_specs=[
                pl.BlockSpec((count, 1, size, size), lambda i, *_: (0, last(i), 0, 0)),
                pl.BlockSpec((one_count, 1, size, size), lambda i, *_: (0, last(i), 0, 0)),
                held(kron.shape),
                held(pool.shape),
                held(left.shape),
            ],
            out_specs=[
                pl.BlockSpec((count, 1, size, size), lambda i, *_: (0, last(i), 0, 0)),
                pl.BlockSpec(
                    (count, 1, size, size),
                    lambda i, *_: (0, jnp.maximum(i - sec_local, 0), 0, 0),
                ),
            ],
            scratch_shapes=[
                pltpu.VMEM((count, size, size), jnp.bfloat16),
                pltpu.VMEM((REACH + 1, count, size, states * size), jnp.bfloat16),
            ],
        ),
        out_shape=[
            jax.ShapeDtypeStruct(operators.shape, jnp.bfloat16),
            jax.ShapeDtypeStruct((count, REACH, size, size), jnp.bfloat16),
        ],
        compiler_params=pltpu.CompilerParams(vmem_limit_bytes=48 * 2**20),
    )(comp_charge, coupling[0], operators, all_ones, kron, pool, left)
    carried = from_behind(carry, "sector", 1)
    return out.at[:, :REACH].add(carried)


def solution(mesh):
    return jax.shard_map(
        body,
        mesh=mesh,
        in_specs=(
            P(None, "sector", "pair", None),
            P("pair", "sector", None, None),
            P("pair", "sector", None, None),
            P("pair", None),
            P("pair"),
            P(),
            P(),
            P(),
        ),
        out_specs=P("pair", "sector", None, None),
        check_vma=False,
    )
```

```python
import jax
import jax.numpy as jnp
from jax import lax
from jax.experimental import pallas as pl
from jax.experimental.pallas import tpu as pltpu
from jax.sharding import PartitionSpec as P

ROWS = 16
REACH = 2


def from_behind(value, axis, steps):
    count = lax.axis_size(axis)
    initial, last = (max(0, -steps), min(count, count - steps))
    return lax.ppermute(value, axis, [(source, source + steps) for source in range(initial, last)])


def renormalize(sec_local, charge, shift, ops, ones, coef, pool, left, out, carry, kron, comb, inner):
    step = pl.program_id(0)
    count, _, size, _ = ops.shape
    one_count = ones.shape[0]
    states = left.shape[0]

    @pl.when(step == 0)
    def _():
        def spread(shape, long, short):
            far = lax.broadcasted_iota(jnp.int32, shape, long)
            near = lax.broadcasted_iota(jnp.int32, shape, short) * ROWS
            inside = jnp.logical_and(far >= near, far < near + ROWS)
            return jnp.where(inside, 1.0, 0.0).astype(jnp.bfloat16)

        tall = jnp.dot(
            spread((count * ROWS, count), 0, 1), coef[...], preferred_element_type=jnp.float32
        ).astype(jnp.bfloat16)
        whole = jnp.dot(
            tall, spread((one_count, one_count * ROWS), 1, 0), preferred_element_type=jnp.float32
        )
        row = lax.broadcasted_iota(jnp.int32, whole.shape, 0) & (ROWS - 1)
        column = lax.broadcasted_iota(jnp.int32, whole.shape, 1) & (ROWS - 1)
        kron[...] = jnp.where(row == column, whole, 0.0).astype(jnp.bfloat16)

    @pl.when(step < sec_local)
    def _():
        for base in range(0, size, 2 * ROWS):
            rows = jnp.concatenate(
                [
                    ones[:, 0, start : start + ROWS, :].reshape(one_count * ROWS, size)
                    for start in (base, base + ROWS)
                ],
                axis=1,
            )
            added = jnp.dot(kron[...], rows, preferred_element_type=jnp.float32)
            for half in range(2):
                start = base + half * ROWS
                part = added[:, half * size : (half + 1) * size].reshape(count, ROWS, size)
                comb[:, start : start + ROWS, :] = (
                    ops[:, 0, start : start + ROWS, :].astype(jnp.float32) + part
                ).astype(jnp.bfloat16)
        slot = lax.rem(step, REACH + 1)

        def one(k, _):
            right = pool[step + charge[k]]
            value = jnp.dot(comb[k], right, preferred_element_type=jnp.float32)
            inner[slot, k] = value.astype(jnp.bfloat16)
            return 0

        lax.fori_loop(0, count, one, 0, unroll=4)

    lefts, slots = [], []
    for t in range(states):
        source = step - shift[t]
        legal = jnp.logical_and(source >= 0, source < sec_local)
        source = jnp.clip(source, 0, sec_local - 1)
        block = left[t, source]
        lefts.append(jnp.where(legal, block, jnp.zeros_like(block)))
        slots.append(lax.rem(source, REACH + 1))
    lhs = jnp.concatenate(lefts, axis=1)

    def emit(target):
        def two(pair, _):
            rhs = jnp.concatenate(
                [
                    jnp.concatenate(
                        [
                            inner[slots[t], 2 * pair + h, :, t * size : (t + 1) * size]
                            for t in range(states)
                        ],
                        axis=0,
                    )
                    for h in range(2)
                ],
                axis=1,
            )
            value = jnp.dot(lhs, rhs, preferred_element_type=jnp.float32)
            for h in range(2):
                target[2 * pair + h, 0] = value[:, h * size : (h + 1) * size].astype(jnp.bfloat16)
            return 0

        lax.fori_loop(0, count // 2, two, 0, unroll=2)

    @pl.when(step < sec_local)
    def _():
        emit(out)

    @pl.when(step >= sec_local)
    def _():
        emit(carry)


def factors(count):
    short = 1 << ((count.bit_length() - 1) // 3)
    return (count // (short * short), short, short)


def gather_both(dims, classes, site, ones, all_site, all_ones, send_sem, recv_sem, own_sem):
    me = lax.axis_index("pair")
    strides = (dims[1] * dims[2], dims[2], 1)
    mine = [lax.rem(lax.div(me, strides[d]), dims[d]) for d in range(3)]

    def moved(place, d, r):
        other = lax.rem(mine[d] + r, dims[d])
        return place + (other - mine[d]) * strides[d]

    barrier = pltpu.get_barrier_semaphore()
    greeted = 0
    for d in range(3):
        for r in range(1, dims[d]):
            pl.semaphore_signal(
                barrier,
                inc=1,
                device_id={"pair": moved(me, d, r)},
                device_id_type=pl.DeviceIdType.MESH,
            )
            greeted += 1
    keep = [
        pltpu.make_async_copy(site, all_site.at[me], own_sem.at[0]),
        pltpu.make_async_copy(ones, all_ones.at[me], own_sem.at[1]),
    ]
    for copy in keep:
        copy.start()
    pl.semaphore_wait(barrier, greeted)

    sent = []

    def piece(c, block, own):
        slabs = classes[c][1]
        if slabs is None:
            return site if own else all_site.at[block]
        part = pl.ds(*slabs)
        return ones.at[part] if own else all_ones.at[block, part]

    def send(c, block, own, stages):
        for d in stages:
            for r in range(1, dims[d]):
                copy = pltpu.make_async_remote_copy(
                    src_ref=piece(c, block, own),
                    dst_ref=piece(c, block, False),
                    send_sem=send_sem.at[len(sent)],
                    recv_sem=recv_sem.at[c, block],
                    device_id={"pair": moved(me, d, r)},
                    device_id_type=pl.DeviceIdType.MESH,
                )
                copy.start()
                sent.append(copy)

    def arrive(c, block):
        pltpu.make_async_remote_copy(
            src_ref=piece(c, block, False),
            dst_ref=piece(c, block, False),
            send_sem=send_sem.at[0],
            recv_sem=recv_sem.at[c, block],
            device_id={"pair": moved(me, 2, 1)},
            device_id_type=pl.DeviceIdType.MESH,
        ).wait_recv()

    for c, (order, _) in enumerate(classes):
        send(c, me, True, order)
    for stage in range(3):
        rounds = []
        for c, (order, _) in enumerate(classes):
            steps = []
            places = [me]
            for d in order[:stage]:
                places = [moved(p, d, r) for r in range(dims[d]) for p in places]
            for r in range(1, dims[order[stage]]):
                steps += [(c, moved(p, order[stage], r)) for p in places]
            rounds.append(steps)
        for i in range(max(len(steps) for steps in rounds)):
            for steps in rounds:
                if i < len(steps):
                    c, block = steps[i]
                    arrive(c, block)
                    send(c, block, False, classes[c][0][stage + 1 :])
    for copy in sent:
        copy.wait_send()
    for copy in keep:
        copy.wait()


def gather(site_tensor, one_index):
    count = lax.axis_size("pair")
    dims = factors(count)
    size = site_tensor.shape[-1]
    site = site_tensor.reshape(-1, size)
    ones = one_index.reshape(-1, size, size)
    slabs = ones.shape[0]
    late = slabs // REACH // 8
    early = (slabs - 2 * late) // 4
    rest = (slabs - 2 * late) // 2 - early
    classes = [((0, 1, 2), None)]
    first = 0
    for order, number in (
        ((0, 1, 2), early),
        ((0, 2, 1), early),
        ((0, 1, 2), rest),
        ((0, 2, 1), slabs - 2 * late - 2 * early - rest),
        ((2, 1, 0), late),
        ((1, 2, 0), late),
    ):
        if number:
            classes.append((order, (first, number)))
        first += number
    all_site, all_ones = pl.pallas_call(
        lambda *refs: gather_both(dims, classes, *refs),
        in_specs=[pl.BlockSpec(memory_space=pl.ANY)] * 2,
        out_specs=[pl.BlockSpec(memory_space=pl.ANY)] * 2,
        out_shape=[
            jax.ShapeDtypeStruct((count,) + site.shape, site.dtype),
            jax.ShapeDtypeStruct((count,) + ones.shape, ones.dtype),
        ],
        scratch_shapes=[
            pltpu.SemaphoreType.DMA((len(classes) * (count - 1),)),
            pltpu.SemaphoreType.DMA((len(classes), count)),
            pltpu.SemaphoreType.DMA((2,)),
        ],
        compiler_params=pltpu.CompilerParams(
            collective_id=0, has_side_effects=True, vmem_limit_bytes=48 * 2**20
        ),
    )(site, ones)
    return (
        all_site.reshape((count,) + site_tensor.shape),
        all_ones.reshape((-1,) + one_index.shape[1:]),
    )


def body(
    site_tensor, operators, one_index, weights, comp_charge, one_charge, sector_size, coupling
):
    count, sec_local, size, _ = operators.shape
    states = site_tensor.shape[0]
    first_sector = lax.axis_index("sector") * sec_local
    gathered_site, all_ones = gather(site_tensor, one_index)
    full_site = jnp.transpose(gathered_site, (1, 2, 0, 3, 4)).reshape(states, sec_local, size, size)
    own_sizes = lax.dynamic_slice_in_dim(sector_size, first_sector, sec_local)
    live_rows = jnp.arange(size, dtype=jnp.int32)[None, :] < own_sizes[:, None]
    own_site = jnp.where(live_rows[None, :, :, None], full_site, jnp.zeros((), jnp.bfloat16))
    upper = from_behind(own_site[:, :REACH], "sector", -1)
    pool = jnp.concatenate([own_site, upper], axis=1)
    pool = jnp.transpose(pool, (1, 2, 0, 3)).reshape(sec_local + REACH, size, states * size)
    left = jnp.swapaxes(own_site, 2, 3)
    matching = comp_charge[:, None] == one_charge[None, :]
    coef = jnp.where(matching, weights, jnp.zeros((), jnp.bfloat16))
    one_count = coef.shape[1]

    def held(shape):
        return pl.BlockSpec(shape, lambda i, *_: (0,) * len(shape))

    def last(i):
        return jnp.minimum(i, sec_local - 1)

    out, carry = pl.pallas_call(
        lambda *refs: renormalize(sec_local, *refs),
        grid_spec=pltpu.PrefetchScalarGridSpec(
            num_scalar_prefetch=2,
            grid=(sec_local + REACH,),
            in_specs=[
                pl.BlockSpec((count, 1, size, size), lambda i, *_: (0, last(i), 0, 0)),
                pl.BlockSpec((one_count, 1, size, size), lambda i, *_: (0, last(i), 0, 0)),
                held(coef.shape),
                held(pool.shape),
                held(left.shape),
            ],
            out_specs=[
                pl.BlockSpec((count, 1, size, size), lambda i, *_: (0, last(i), 0, 0)),
                pl.BlockSpec(
                    (count, 1, size, size),
                    lambda i, *_: (0, jnp.maximum(i - sec_local, 0), 0, 0),
                ),
            ],
            scratch_shapes=[
                pltpu.VMEM((count * ROWS, one_count * ROWS), jnp.bfloat16),
                pltpu.VMEM((count, size, size), jnp.bfloat16),
                pltpu.VMEM((REACH + 1, count, size, states * size), jnp.bfloat16),
            ],
        ),
        out_shape=[
            jax.ShapeDtypeStruct(operators.shape, jnp.bfloat16),
            jax.ShapeDtypeStruct((count, REACH, size, size), jnp.bfloat16),
        ],
        compiler_params=pltpu.CompilerParams(vmem_limit_bytes=48 * 2**20),
    )(comp_charge, coupling[0], operators, all_ones, coef, pool, left)
    carried = from_behind(carry, "sector", 1)
    return out.at[:, :REACH].add(carried)


def solution(mesh):
    return jax.shard_map(
        body,
        mesh=mesh,
        in_specs=(
            P(None, "sector", "pair", None),
            P("pair", "sector", None, None),
            P("pair", "sector", None, None),
            P("pair", None),
            P("pair"),
            P(),
            P(),
            P(),
        ),
        out_specs=P("pair", "sector", None, None),
        check_vma=False,
    )
```

```python
import jax
import jax.numpy as jnp
from jax import lax
from jax.experimental import pallas as pl
from jax.experimental.pallas import tpu as pltpu
from jax.sharding import PartitionSpec as P

ROWS = 16
REACH = 2


def from_behind(value, axis, steps):
    count = lax.axis_size(axis)
    initial, last = (max(0, -steps), min(count, count - steps))
    return lax.ppermute(value, axis, [(source, source + steps) for source in range(initial, last)])


def renormalize(sec_local, charge, shift, ops, ones, coef, pool, left, out, carry, kron, comb, inner):
    step = pl.program_id(0)
    count, _, size, _ = ops.shape
    one_count = ones.shape[0]
    states = left.shape[0]

    @pl.when(step == 0)
    def _():
        def spread(shape, long, short):
            far = lax.broadcasted_iota(jnp.int32, shape, long)
            near = lax.broadcasted_iota(jnp.int32, shape, short) * ROWS
            inside = jnp.logical_and(far >= near, far < near + ROWS)
            return jnp.where(inside, 1.0, 0.0).astype(jnp.bfloat16)

        tall = jnp.dot(
            spread((count * ROWS, count), 0, 1), coef[...], preferred_element_type=jnp.float32
        ).astype(jnp.bfloat16)
        whole = jnp.dot(
            tall, spread((one_count, one_count * ROWS), 1, 0), preferred_element_type=jnp.float32
        )
        row = lax.broadcasted_iota(jnp.int32, whole.shape, 0) & (ROWS - 1)
        column = lax.broadcasted_iota(jnp.int32, whole.shape, 1) & (ROWS - 1)
        kron[...] = jnp.where(row == column, whole, 0.0).astype(jnp.bfloat16)

    @pl.when(step < sec_local)
    def _():
        for base in range(0, size, 2 * ROWS):
            rows = jnp.concatenate(
                [
                    ones[:, 0, start : start + ROWS, :].reshape(one_count * ROWS, size)
                    for start in (base, base + ROWS)
                ],
                axis=1,
            )
            added = jnp.dot(kron[...], rows, preferred_element_type=jnp.float32)
            for half in range(2):
                start = base + half * ROWS
                part = added[:, half * size : (half + 1) * size].reshape(count, ROWS, size)
                comb[:, start : start + ROWS, :] = (
                    ops[:, 0, start : start + ROWS, :].astype(jnp.float32) + part
                ).astype(jnp.bfloat16)
        slot = lax.rem(step, REACH + 1)

        def one(k, _):
            right = pool[step + charge[k]]
            value = jnp.dot(comb[k], right, preferred_element_type=jnp.float32)
            inner[slot, k] = value.astype(jnp.bfloat16)
            return 0

        lax.fori_loop(0, count, one, 0, unroll=4)

    lefts, slots = [], []
    for t in range(states):
        source = step - shift[t]
        legal = jnp.logical_and(source >= 0, source < sec_local)
        source = jnp.clip(source, 0, sec_local - 1)
        block = left[t, source]
        lefts.append(jnp.where(legal, block, jnp.zeros_like(block)))
        slots.append(lax.rem(source, REACH + 1))
    lhs = jnp.concatenate(lefts, axis=1)

    def emit(target):
        def two(pair, _):
            rhs = jnp.concatenate(
                [
                    jnp.concatenate(
                        [
                            inner[slots[t], 2 * pair + h, :, t * size : (t + 1) * size]
                            for t in range(states)
                        ],
                        axis=0,
                    )
                    for h in range(2)
                ],
                axis=1,
            )
            value = jnp.dot(lhs, rhs, preferred_element_type=jnp.float32)
            for h in range(2):
                target[2 * pair + h, 0] = value[:, h * size : (h + 1) * size].astype(jnp.bfloat16)
            return 0

        lax.fori_loop(0, count // 2, two, 0, unroll=2)

    @pl.when(step < sec_local)
    def _():
        emit(out)

    @pl.when(step >= sec_local)
    def _():
        emit(carry)


def factors(count):
    short = 1 << ((count.bit_length() - 1) // 3)
    return (count // (short * short), short, short)


def gather_both(dims, classes, site, ones, all_site, all_ones, send_sem, recv_sem, own_sem):
    me = lax.axis_index("pair")
    strides = (dims[1] * dims[2], dims[2], 1)
    mine = [lax.rem(lax.div(me, strides[d]), dims[d]) for d in range(3)]

    def moved(place, d, r):
        other = lax.rem(mine[d] + r, dims[d])
        return place + (other - mine[d]) * strides[d]

    barrier = pltpu.get_barrier_semaphore()
    greeted = 0
    for d in range(3):
        for r in range(1, dims[d]):
            pl.semaphore_signal(
                barrier,
                inc=1,
                device_id={"pair": moved(me, d, r)},
                device_id_type=pl.DeviceIdType.MESH,
            )
            greeted += 1
    keep = [
        pltpu.make_async_copy(site, all_site.at[me], own_sem.at[0]),
        pltpu.make_async_copy(ones, all_ones.at[me], own_sem.at[1]),
    ]
    for copy in keep:
        copy.start()
    pl.semaphore_wait(barrier, greeted)

    sent = []

    def piece(c, block, own):
        slabs = classes[c][1]
        if slabs is None:
            return site if own else all_site.at[block]
        part = pl.ds(*slabs)
        return ones.at[part] if own else all_ones.at[block, part]

    def send(c, block, own, stages):
        for d in stages:
            for r in range(1, dims[d]):
                copy = pltpu.make_async_remote_copy(
                    src_ref=piece(c, block, own),
                    dst_ref=piece(c, block, False),
                    send_sem=send_sem.at[len(sent)],
                    recv_sem=recv_sem.at[c, block],
                    device_id={"pair": moved(me, d, r)},
                    device_id_type=pl.DeviceIdType.MESH,
                )
                copy.start()
                sent.append(copy)

    def arrive(c, block):
        pltpu.make_async_remote_copy(
            src_ref=piece(c, block, False),
            dst_ref=piece(c, block, False),
            send_sem=send_sem.at[0],
            recv_sem=recv_sem.at[c, block],
            device_id={"pair": moved(me, 2, 1)},
            device_id_type=pl.DeviceIdType.MESH,
        ).wait_recv()

    for c, (order, _) in enumerate(classes):
        send(c, me, True, order)
    for stage in range(3):
        rounds = []
        for c, (order, _) in enumerate(classes):
            steps = []
            places = [me]
            for d in order[:stage]:
                places = [moved(p, d, r) for r in range(dims[d]) for p in places]
            for r in range(1, dims[order[stage]]):
                steps += [(c, moved(p, order[stage], r)) for p in places]
            rounds.append(steps)
        for i in range(max(len(steps) for steps in rounds)):
            for steps in rounds:
                if i < len(steps):
                    c, block = steps[i]
                    arrive(c, block)
                    send(c, block, False, classes[c][0][stage + 1 :])
    for copy in sent:
        copy.wait_send()
    for copy in keep:
        copy.wait()


def gather(site_tensor, one_index):
    count = lax.axis_size("pair")
    dims = factors(count)
    size = site_tensor.shape[-1]
    site = site_tensor.reshape(-1, size)
    ones = one_index.reshape(-1, size, size)
    slabs = ones.shape[0]
    late = slabs // 8
    early = (slabs - 2 * late) // 2
    classes = [((0, 1, 2), None)]
    first = 0
    for order, number in (
        ((0, 1, 2), early),
        ((0, 2, 1), slabs - 2 * late - early),
        ((2, 1, 0), late),
        ((1, 2, 0), late),
    ):
        if number:
            classes.append((order, (first, number)))
        first += number
    all_site, all_ones = pl.pallas_call(
        lambda *refs: gather_both(dims, classes, *refs),
        in_specs=[pl.BlockSpec(memory_space=pl.ANY)] * 2,
        out_specs=[pl.BlockSpec(memory_space=pl.ANY)] * 2,
        out_shape=[
            jax.ShapeDtypeStruct((count,) + site.shape, site.dtype),
            jax.ShapeDtypeStruct((count,) + ones.shape, ones.dtype),
        ],
        scratch_shapes=[
            pltpu.SemaphoreType.DMA((len(classes) * (count - 1),)),
            pltpu.SemaphoreType.DMA((len(classes), count)),
            pltpu.SemaphoreType.DMA((2,)),
        ],
        compiler_params=pltpu.CompilerParams(
            collective_id=0, has_side_effects=True, vmem_limit_bytes=48 * 2**20
        ),
    )(site, ones)
    return (
        all_site.reshape((count,) + site_tensor.shape),
        all_ones.reshape((-1,) + one_index.shape[1:]),
    )


def body(
    site_tensor, operators, one_index, weights, comp_charge, one_charge, sector_size, coupling
):
    count, sec_local, size, _ = operators.shape
    states = site_tensor.shape[0]
    first_sector = lax.axis_index("sector") * sec_local
    gathered_site, all_ones = gather(site_tensor, one_index)
    full_site = jnp.transpose(gathered_site, (1, 2, 0, 3, 4)).reshape(states, sec_local, size, size)
    own_sizes = lax.dynamic_slice_in_dim(sector_size, first_sector, sec_local)
    live_rows = jnp.arange(size, dtype=jnp.int32)[None, :] < own_sizes[:, None]
    own_site = jnp.where(live_rows[None, :, :, None], full_site, jnp.zeros((), jnp.bfloat16))
    upper = from_behind(own_site[:, :REACH], "sector", -1)
    pool = jnp.concatenate([own_site, upper], axis=1)
    pool = jnp.transpose(pool, (1, 2, 0, 3)).reshape(sec_local + REACH, size, states * size)
    left = jnp.swapaxes(own_site, 2, 3)
    matching = comp_charge[:, None] == one_charge[None, :]
    coef = jnp.where(matching, weights, jnp.zeros((), jnp.bfloat16))
    one_count = coef.shape[1]

    def held(shape):
        return pl.BlockSpec(shape, lambda i, *_: (0,) * len(shape))

    def last(i):
        return jnp.minimum(i, sec_local - 1)

    out, carry = pl.pallas_call(
        lambda *refs: renormalize(sec_local, *refs),
        grid_spec=pltpu.PrefetchScalarGridSpec(
            num_scalar_prefetch=2,
            grid=(sec_local + REACH,),
            in_specs=[
                pl.BlockSpec((count, 1, size, size), lambda i, *_: (0, last(i), 0, 0)),
                pl.BlockSpec((one_count, 1, size, size), lambda i, *_: (0, last(i), 0, 0)),
                held(coef.shape),
                held(pool.shape),
                held(left.shape),
            ],
            out_specs=[
                pl.BlockSpec((count, 1, size, size), lambda i, *_: (0, last(i), 0, 0)),
                pl.BlockSpec(
                    (count, 1, size, size),
                    lambda i, *_: (0, jnp.maximum(i - sec_local, 0), 0, 0),
                ),
            ],
            scratch_shapes=[
                pltpu.VMEM((count * ROWS, one_count * ROWS), jnp.bfloat16),
                pltpu.VMEM((count, size, size), jnp.bfloat16),
                pltpu.VMEM((REACH + 1, count, size, states * size), jnp.bfloat16),
            ],
        ),
        out_shape=[
            jax.ShapeDtypeStruct(operators.shape, jnp.bfloat16),
            jax.ShapeDtypeStruct((count, REACH, size, size), jnp.bfloat16),
        ],
        compiler_params=pltpu.CompilerParams(vmem_limit_bytes=48 * 2**20),
    )(comp_charge, coupling[0], operators, all_ones, coef, pool, left)
    carried = from_behind(carry, "sector", 1)
    return out.at[:, :REACH].add(carried)


def solution(mesh):
    return jax.shard_map(
        body,
        mesh=mesh,
        in_specs=(
            P(None, "sector", "pair", None),
            P("pair", "sector", None, None),
            P("pair", "sector", None, None),
            P("pair", None),
            P("pair"),
            P(),
            P(),
            P(),
        ),
        out_specs=P("pair", "sector", None, None),
        check_vma=False,
    )
```
